512 devices in a mesh: ma: 8 (over x, z_lo), ka: 16 (over y, core), an: 4 (over z_hi).
Axes of the slice: x: 4, y: 8, z: 8 (z_hi: 4, z_lo: 2; z = z_hi * 2 + z_lo), core: 2. Of those that a mesh axis runs over, the one named last changes fastest.
Arguments:
- left_matrix: float32 [16384, 16384], P('ma', 'ka'), may hold values from -6 to 6
- right_panel: float32 [16384, 2048], P(('ka', 'ma'), 'an'), may hold values from -0.046875 to 0.046875
Outputs:
- product_panel: float32 [16384, 2048], P(('ma', 'ka'), 'an')
The draws below stay inside these ranges and needn't reach their ends.
All inputs are finite; a program needn't handle non-finite values.
Results may differ from the reference program's by a relative error of at most 0.000073.
Values sent between devices are 32-bit elements; how exact they have to be, the bound alone decides.
No kernel may reach another device: no remote copies, remote signals or barrier semaphores. Data moves between devices by JAX's collectives and lax.ppermute only.
A program may use at most 64 MiB of HBM per device.

```python
import jax
import jax.numpy as jnp
from jax import lax

KDIM = 16384
NCOL = 2048
MROWS = 16384


def strengthened(array, key, source, target, shards_of, factor):
    owner, partner = [(jnp.arange(array.shape[position]) // (array.shape[position] // shards_of)).reshape([-1 if axis == position else 1 for axis in range(array.ndim)]) for position in (source, target)]
    chosen = jax.random.permutation(key, shards_of)[partner]
    strong = (owner == chosen) | (owner == (partner + shards_of // 2) % shards_of)
    return jnp.where(strong, factor * array, array)


def block_levels(own_key, dims, split, smallest, largest):
    factor_of, own = 1.0, jax.random.fold_in(own_key, 6)
    for dim, shards_of in split:
        draws = jnp.exp(jax.random.uniform(jax.random.fold_in(own, dim), (shards_of,), jnp.float32, smallest / len(split), largest / len(split)))
        factor_of = factor_of * jnp.repeat(draws, dims[dim] // shards_of).reshape([-1 if axis == dim else 1 for axis in range(len(dims))])
    return factor_of


def noise(key, shape, spread, bound, split=(), kind=jnp.bfloat16):
    values = spread * jax.random.normal(key, shape, jnp.float32)
    if split:
        values = values * block_levels(key, shape, split, -0.22, 0.18)
    return jnp.clip(values, -bound, bound).astype(kind)


def gaussian_with(stream_key, extent, scale, bound, split, heavy, held_as=jnp.bfloat16):
    drawn = scale * jax.random.normal(stream_key, extent, jnp.float32)
    if split:
        drawn = drawn * block_levels(stream_key, extent, split, -0.22, 0.18)
    return jnp.clip(strengthened(drawn, jax.random.fold_in(stream_key, 3), *heavy), -bound, bound).astype(held_as)


def setup_inputs(seed: int = 0) -> dict:
    streams_of = jax.random.split(jax.random.key(seed), 3)
    return {
        "left_matrix": gaussian_with(streams_of[0], (MROWS, KDIM), 1.0, 6.0, ((0, 8), (1, 16)), (1, 0, 16, 2.0), jnp.float32),
        "right_panel": noise(streams_of[1], (KDIM, NCOL), KDIM ** -0.5, 0.046875, ((0, 128), (1, 4)), jnp.float32),
    }


def reference(left_matrix, right_panel):
    return jnp.dot(left_matrix, right_panel, preferred_element_type=jnp.float32, precision=lax.Precision.HIGHEST)
```

```python
import jax
import jax.numpy as jnp
from jax import lax
from jax.experimental import pallas as pl
from jax.experimental.pallas import tpu as pltpu
from jax.sharding import PartitionSpec as P

F32, BF16 = jnp.float32, jnp.bfloat16
VMEM_LIMIT = 48 * 1024 * 1024


def params():
    return pltpu.CompilerParams(vmem_limit_bytes=VMEM_LIMIT)


def two_parts(value):
    high = value.astype(BF16)
    return high, (value - high.astype(F32)).astype(BF16)


def split_kernel(a_ref, high_ref, low_ref):
    high_ref[...], low_ref[...] = two_parts(a_ref[...])


def split(a):
    rows, cols = a.shape
    spec = pl.BlockSpec((256, cols), lambda i: (i, 0))
    return pl.pallas_call(
        split_kernel,
        grid=(rows // 256,),
        in_specs=[spec],
        out_specs=[spec, spec],
        out_shape=[jax.ShapeDtypeStruct(a.shape, BF16)] * 2,
        compiler_params=params(),
        cost_estimate=pl.CostEstimate(flops=4 * rows * cols, bytes_accessed=8 * rows * cols, transcendentals=0),
    )(a)


def split_b_kernel(place, b_ref, high_ref, low_ref):
    core = place[1]
    for slot in range(2):
        block = b_ref[:, core if slot == 0 else 1 - core].reshape(1024, 256)
        high_ref[slot], low_ref[slot] = two_parts(block)


def split_b(place, gathered):
    return pl.pallas_call(
        split_b_kernel,
        grid_spec=pltpu.PrefetchScalarGridSpec(
            num_scalar_prefetch=1,
            in_specs=[pl.BlockSpec(memory_space=pltpu.VMEM)],
            out_specs=[pl.BlockSpec(memory_space=pltpu.VMEM)] * 2,
        ),
        out_shape=[jax.ShapeDtypeStruct((2, 1024, 256), BF16)] * 2,
        compiler_params=params(),
        cost_estimate=pl.CostEstimate(flops=2 << 20, bytes_accessed=4 << 20, transcendentals=0),
    )(place, gathered)


def product_kernel(count, place, own_high, own_low, other_high, other_low, b_high, b_low, *outs):
    step = pl.program_id(0)

    def dot(a_ref, b):
        return jnp.dot(a_ref[...], b, preferred_element_type=F32)

    total = dot(own_high, b_low[0]) + dot(own_low, b_high[0])
    total += dot(other_high, b_low[1]) + dot(other_low, b_high[1])
    total += dot(own_high, b_high[0]) + dot(other_high, b_high[1])
    for index, out in enumerate(outs):

        @pl.when(step == index)
        def _(out=out):
            out[...] = total


def products(place, shifts, parts, b_high, b_low):
    count = len(shifts)

    def chosen(i, place):
        shift = shifts[0]
        for index in range(1, count):
            shift = jnp.where(i == index, shifts[index], shift)
        return ((place[0] + shift) % 8, 0)

    a_spec = pl.BlockSpec((256, 1024), chosen)
    whole = pl.BlockSpec(memory_space=pltpu.VMEM)
    flops = 2 * 3 * 256 * 2048 * 256 * count
    return pl.pallas_call(
        lambda *refs: product_kernel(count, *refs),
        grid_spec=pltpu.PrefetchScalarGridSpec(
            num_scalar_prefetch=1,
            grid=(count,),
            in_specs=[a_spec] * 4 + [whole] * 2,
            out_specs=[whole] * count,
        ),
        out_shape=[jax.ShapeDtypeStruct((256, 256), F32)] * count,
        compiler_params=params(),
        cost_estimate=pl.CostEstimate(flops=flops, bytes_accessed=count * (2 << 20), transcendentals=0),
    )(place, *parts, b_high, b_low)


def along_y(distance):
    return [(i, (i + 2 * distance) % 16) for i in range(16)]


def by_core(distance):
    return [(i, (i + (2 * distance if i % 2 == 0 else -2 * distance)) % 16) for i in range(16)]


CORES = [(i, i ^ 1) for i in range(16)]
PLANES = [[m * 16 + 2 * y + c for m in range(8) for c in range(2)] for y in range(8)]


def shards(left_matrix, right_panel):
    ka = lax.axis_index("ka")
    y, core = ka // 2, ka % 2
    place = jnp.stack([y, core]).astype(jnp.int32)

    halves = right_panel.reshape(128, 2, 256).transpose(1, 0, 2)
    sent = jnp.broadcast_to(halves[None], (8, 2, 128, 256)).reshape(16, 128, 256)
    gathered = lax.all_to_all(sent, ("ma", "ka"), 0, 0, axis_index_groups=PLANES).reshape(8, 2, 128, 256)
    other = lax.ppermute(left_matrix, "ka", CORES)

    parts = [*split(left_matrix), *split(other)]
    b_high, b_low = split_b(place, gathered)

    up3, down3, four = products(place, (3, -3, 4), parts, b_high, b_low)
    got_up3 = lax.ppermute(up3, "ka", along_y(1))
    got_down3 = lax.ppermute(down3, "ka", along_y(-1))
    got_four = lax.ppermute(four, "ka", by_core(2))
    up1, down1, up2, down2, mine = products(place, (1, -1, 2, -2, 0), parts, b_high, b_low)
    got_up1 = lax.ppermute(up1, "ka", along_y(1))
    got_down1 = lax.ppermute(down1, "ka", along_y(-1))

    up2 = up2 + got_up3 + jnp.where(core == 0, got_four, 0.0)
    down2 = down2 + got_down3 + jnp.where(core == 1, got_four, 0.0)
    got_up2 = lax.ppermute(up2, "ka", along_y(2))
    got_down2 = lax.ppermute(down2, "ka", along_y(-2))

    total = (mine + got_up1 + got_down1 + got_up2 + got_down2).reshape(2, 128, 256)
    keep = jnp.where(core == 0, total[0], total[1])
    give = jnp.where(core == 0, total[1], total[0])
    got = lax.ppermute(give, "ka", CORES)
    return jnp.concatenate([jnp.where(core == 0, keep, got), jnp.where(core == 0, got, keep)], axis=1)


def solution(mesh):
    in_specs = (P("ma", "ka"), P(("ka", "ma"), "an"))
    out_specs = P(("ma", "ka"), "an")
    return jax.shard_map(shards, mesh=mesh, in_specs=in_specs, out_specs=out_specs, check_vma=False)
```

```python
import jax
import jax.numpy as jnp
from jax import lax
from jax.experimental import pallas as pl
from jax.experimental.pallas import tpu as pltpu
from jax.sharding import PartitionSpec as P

F32, BF16 = jnp.float32, jnp.bfloat16
VMEM = pl.BlockSpec(memory_space=pltpu.VMEM)
MIB = 1024 * 1024


def two_parts(value):
    high = value.astype(BF16)
    return high, (value - high.astype(F32)).astype(BF16)


def place():
    ka, ma = lax.axis_index("ka"), lax.axis_index("ma")
    return ka // 2, ka % 2, ma % 2, ma // 2


def dot(a, b):
    return jnp.dot(a, b, preferred_element_type=F32)


def early_kernel(a_ref, b0, b1, b2, b3, sums, high_out, low_out, b_high, b_low):
    _, _, half, own_x = place()
    for index, b_ref in enumerate((b0, b1, b2, b3)):
        rows = slice(128 * index, 128 * index + 128)
        b_high[rows, :], b_low[rows, :] = two_parts(b_ref[...])

    def body(a_block, sums_block, high_block, low_block):
        def parts(z):
            starts = [pl.multiple_of((2 * ((own_x + offset) % 4) + z) * 128, 128) for offset in OFFSETS]
            return two_parts(jnp.concatenate([a_block[:, pl.ds(start, 128)] for start in starts], axis=1))

        high, low = parts(half)
        sums_block[...] = dot(high, b_low[...]) + dot(low, b_high[...]) + dot(high, b_high[...])
        high_block[...], low_block[...] = parts(1 - half)

    spec = pl.BlockSpec((256, 512), lambda i: (i, 0))
    pltpu.emit_pipeline(
        body, grid=(8,), in_specs=[pl.BlockSpec((256, 1024), lambda i: (i, 0))], out_specs=[spec] * 3
    )(a_ref, sums, high_out, low_out)


def early(a, near_b):
    return pl.pallas_call(
        early_kernel,
        in_specs=[pl.BlockSpec(memory_space=pltpu.HBM)] + [VMEM] * 4,
        out_specs=[pl.BlockSpec(memory_space=pl.ANY)] * 3,
        out_shape=[jax.ShapeDtypeStruct((2048, 512), kind) for kind in (F32, BF16, BF16)],
        scratch_shapes=[pltpu.VMEM((512, 512), BF16)] * 2,
        compiler_params=pltpu.CompilerParams(vmem_limit_bytes=12 * MIB),
        cost_estimate=pl.CostEstimate(flops=2 * 3 * 2048 * 512 * 512, bytes_accessed=16 * MIB, transcendentals=0),
    )(a, *near_b)


def late_kernel(shifts, mine, a_high, a_low, early_ref, b0, b1, b2, b3, out, b_high, b_low):
    y, core, _, _ = place()
    side = core if mine else 1 - core
    for index, b_ref in enumerate((b0, b1, b2, b3)):
        rows = slice(128 * index, 128 * index + 128)
        b_high[rows, :], b_low[rows, :] = two_parts(b_ref[...])
    at = 0
    for shift in shifts:
        if shift in (0, 4):
            start, count = ((y + shift) % 8) * 256 + side * 128, 128
        else:
            start, count = ((y + jnp.where(side == 0, shift, 8 - shift)) % 8) * 256, 256
        rows = pl.ds(pl.multiple_of(start, 128), count)
        high, low = a_high[rows, :], a_low[rows, :]
        total = dot(high, b_low[...]) + dot(low, b_high[...]) + dot(high, b_high[...])
        out[at : at + count, :] = early_ref[rows, :] + total
        at += count


def late(shifts, mine, a_high, a_low, sums, far_b):
    count = sum(128 if shift in (0, 4) else 256 for shift in shifts)
    return pl.pallas_call(
        lambda *refs: late_kernel(shifts, mine, *refs),
        in_specs=[VMEM] * 7,
        out_specs=VMEM,
        out_shape=jax.ShapeDtypeStruct((count, 512), F32),
        scratch_shapes=[pltpu.VMEM((512, 512), BF16)] * 2,
        compiler_params=pltpu.CompilerParams(vmem_limit_bytes=14 * MIB),
        cost_estimate=pl.CostEstimate(flops=2 * 3 * count * 512 * 512, bytes_accessed=10 * MIB, transcendentals=0),
    )(a_high, a_low, sums, *far_b)


def add_kernel(first, second, *outs):
    at = 0
    for out in outs:
        rows = slice(at, at + out.shape[0])
        out[...] = first[rows, :] + second[rows, :]
        at += out.shape[0]


def add(first, second, *counts):
    return pl.pallas_call(
        add_kernel,
        in_specs=[VMEM] * 2,
        out_specs=[VMEM] * len(counts),
        out_shape=[jax.ShapeDtypeStruct((count, 512), F32) for count in counts],
        compiler_params=pltpu.CompilerParams(vmem_limit_bytes=6 * MIB),
        cost_estimate=pl.CostEstimate(flops=MIB, bytes_accessed=4 * MIB, transcendentals=0),
    )(first, second)


def pass_on_kernel(two, got_three, got_four, own, other):
    _, core, _, _ = place()
    for index, out in ((core, own), (1 - core, other)):
        rows = pl.ds(pl.multiple_of(index * 128, 128), 128)
        total = two[rows, :] + got_three[rows, :]
        out[...] = total + got_four[...] if out is own else total


def here_kernel(zero, got_one, keep, give):
    _, core, _, _ = place()
    keep[...] = zero[...] + got_one[pl.ds(pl.multiple_of(core * 128, 128), 128), :]
    give[...] = got_one[pl.ds(pl.multiple_of((1 - core) * 128, 128), 128), :]


def halves(kernel, *args):
    return pl.pallas_call(
        kernel,
        in_specs=[VMEM] * len(args),
        out_specs=[VMEM] * 2,
        out_shape=[jax.ShapeDtypeStruct((128, 512), F32)] * 2,
        compiler_params=pltpu.CompilerParams(vmem_limit_bytes=4 * MIB),
        cost_estimate=pl.CostEstimate(flops=MIB, bytes_accessed=2 * MIB, transcendentals=0),
    )(*args)


def along_y(distance, cross=0):
    return [(i, ((i + (2 * distance if i % 2 == 0 else -2 * distance)) % 16) ^ cross) for i in range(16)]


CORES = [(i, i ^ 1) for i in range(16)]
HALVES = [(i, i ^ 1) for i in range(8)]


FAR, NEAR = (3, 1, 4), (2, 0)
OFFSETS = (0, -1, 1, 2)


def by_x(offset):
    pairs = []
    for ma in range(8):
        for ka in range(16):
            step = 2 if offset == 2 and ka % 2 == 0 else -offset
            pairs.append((ma * 16 + ka, ((ma + 2 * step) % 8) * 16 + ka))
    return pairs


def shards(left_matrix, right_panel):
    def from_row(b):
        return [b] + [lax.ppermute(b, ("ma", "ka"), by_x(offset)) for offset in OFFSETS[1:]]

    far_b = from_row(lax.ppermute(right_panel, "ma", HALVES))
    sums, a_high, a_low = early(left_matrix, from_row(right_panel))

    def rest(shifts, mine, sums):
        return late(shifts, mine, a_high, a_low, sums, far_b)

    three, one, four = add(lax.ppermute(rest(FAR, False, sums), "ka", CORES), rest(FAR, True, sums), 256, 256, 128)
    sent = rest(NEAR, False, sums)
    three, four, one, sent, sums = lax.optimization_barrier((three, four, one, sent, sums))
    got_three = lax.ppermute(three, "ka", along_y(1))
    got_four = lax.ppermute(four, "ka", along_y(2))
    got_one = lax.ppermute(one, "ka", along_y(1))
    two, zero = add(lax.ppermute(sent, "ka", CORES), rest(NEAR, True, sums), 256, 128)

    own, other = halves(pass_on_kernel, two, got_three, got_four)
    got_own = lax.ppermute(own, "ka", along_y(2))
    got_other = lax.ppermute(other, "ka", along_y(2, 1))

    keep, give = halves(here_kernel, zero, got_one)
    got_give = lax.ppermute(give, "ka", CORES)
    return keep + got_give + got_own + got_other


def solution(mesh):
    in_specs = (P("ma", "ka"), P(("ka", "ma"), "an"))
    out_specs = P(("ma", "ka"), "an")
    return jax.shard_map(shards, mesh=mesh, in_specs=in_specs, out_specs=out_specs, check_vma=False)
```

```python
import jax
import jax.numpy as jnp
from jax import lax
from jax.experimental import pallas as pl
from jax.experimental.pallas import tpu as pltpu
from jax.sharding import PartitionSpec as P

F32, BF16 = jnp.float32, jnp.bfloat16
VMEM = pl.BlockSpec(memory_space=pltpu.VMEM)
MIB = 1024 * 1024


def two_parts(value):
    high = value.astype(BF16)
    return high, (value - high.astype(F32)).astype(BF16)


def place():
    ka, ma = lax.axis_index("ka"), lax.axis_index("ma")
    return ka // 2, ka % 2, ma % 2, ma // 2


def dot(a, b):
    return jnp.dot(a, b, preferred_element_type=F32)


def place_parts(pieces, high, low):
    _, _, _, own_x = place()
    for offset, piece in zip(OFFSETS, pieces):
        rows = pl.ds(pl.multiple_of(((own_x + offset) % 4) * 128, 128), 128)
        high[rows, :], low[rows, :] = two_parts(piece[...])


def early_kernel(a_hbm, b0_hbm, b1, b2, b3, sums, high_out, low_out, a_ref, b0, b_high, b_low, a_sems, b_sem):
    _, _, half, _ = place()

    def load(step):
        return pltpu.make_async_copy(a_hbm.at[pl.ds(256 * step, 256)], a_ref.at[step], a_sems.at[step])

    b_load = pltpu.make_async_copy(b0_hbm, b0, b_sem)
    b_load.start()
    for step in range(8):
        load(step).start()
    b_load.wait()
    place_parts((b0, b1, b2, b3), b_high, b_low)
    for z in range(2):

        @pl.when(half == z)
        def _(z=z):
            @pl.loop(0, 8)
            def _(step):
                load(step).wait()

                def parts(z):
                    blocks = [a_ref[step, :, 256 * x + 128 * z : 256 * x + 128 * z + 128] for x in range(4)]
                    return two_parts(jnp.concatenate(blocks, axis=1))

                rows = pl.ds(pl.multiple_of(256 * step, 256), 256)
                high, low = parts(z)
                sums[rows, :] = dot(high, b_low[...]) + dot(low, b_high[...]) + dot(high, b_high[...])
                high_out[rows, :], low_out[rows, :] = parts(1 - z)


def early(a, near_b):
    kept = pl.BlockSpec(memory_space=pl.ANY)
    return pl.pallas_call(
        early_kernel,
        in_specs=[kept] * 2 + [VMEM] * 3,
        out_specs=[VMEM] * 3,
        out_shape=[jax.ShapeDtypeStruct((2048, 512), kind) for kind in (F32, BF16, BF16)],
        scratch_shapes=[
            pltpu.VMEM((8, 256, 1024), F32),
            pltpu.VMEM((128, 512), F32),
            pltpu.VMEM((512, 512), BF16),
            pltpu.VMEM((512, 512), BF16),
            pltpu.SemaphoreType.DMA((8,)),
            pltpu.SemaphoreType.DMA,
        ],
        compiler_params=pltpu.CompilerParams(vmem_limit_bytes=42 * MIB),
        cost_estimate=pl.CostEstimate(flops=2 * 3 * 2048 * 512 * 512, bytes_accessed=16 * MIB, transcendentals=0),
    )(a, *near_b)


def late_kernel(shifts, mine, a_high, a_low, early_ref, b0, b1, b2, b3, out, b_high, b_low):
    y, core, _, _ = place()
    side = core if mine else 1 - core
    place_parts((b0, b1, b2, b3), b_high, b_low)
    at = 0
    for shift in shifts:
        if shift in (0, 4):
            start, count = ((y + shift) % 8) * 256 + side * 128, 128
        else:
            start, count = ((y + jnp.where(side == 0, shift, 8 - shift)) % 8) * 256, 256
        rows = pl.ds(pl.multiple_of(start, 128), count)
        high, low = a_high[rows, :], a_low[rows, :]
        total = dot(high, b_low[...]) + dot(low, b_high[...]) + dot(high, b_high[...])
        out[at : at + count, :] = early_ref[rows, :] + total
        at += count


def late(shifts, mine, a_high, a_low, sums, far_b):
    count = sum(128 if shift in (0, 4) else 256 for shift in shifts)
    return pl.pallas_call(
        lambda *refs: late_kernel(shifts, mine, *refs),
        in_specs=[VMEM] * 7,
        out_specs=VMEM,
        out_shape=jax.ShapeDtypeStruct((count, 512), F32),
        scratch_shapes=[pltpu.VMEM((512, 512), BF16)] * 2,
        compiler_params=pltpu.CompilerParams(vmem_limit_bytes=14 * MIB),
        cost_estimate=pl.CostEstimate(flops=2 * 3 * count * 512 * 512, bytes_accessed=10 * MIB, transcendentals=0),
    )(a_high, a_low, sums, *far_b)


def add_kernel(first, second, three, four, one_own, one_other, two, zero):
    _, core, _, _ = place()
    own, other = (pl.multiple_of(256 + side * 128, 128) for side in (core, 1 - core))
    for start, out in ((0, three), (own, one_own), (other, one_other), (512, four), (640, two), (896, zero)):
        rows = pl.ds(start, out.shape[0])
        out[...] = first[rows, :] + second[rows, :]


def add(first, second):
    counts = (256, 128, 128, 128, 256, 128)
    return pl.pallas_call(
        add_kernel,
        in_specs=[VMEM] * 2,
        out_specs=[VMEM] * len(counts),
        out_shape=[jax.ShapeDtypeStruct((count, 512), F32) for count in counts],
        compiler_params=pltpu.CompilerParams(vmem_limit_bytes=8 * MIB),
        cost_estimate=pl.CostEstimate(flops=MIB, bytes_accessed=4 * MIB, transcendentals=0),
    )(first, second)


def pass_on_kernel(two, got_three, got_four, own, other):
    _, core, _, _ = place()
    for index, out in ((core, own), (1 - core, other)):
        rows = pl.ds(pl.multiple_of(index * 128, 128), 128)
        total = two[rows, :] + got_three[rows, :]
        out[...] = total + got_four[...] if out is own else total


def halves(kernel, *args):
    return pl.pallas_call(
        kernel,
        in_specs=[VMEM] * len(args),
        out_specs=[VMEM] * 2,
        out_shape=[jax.ShapeDtypeStruct((128, 512), F32)] * 2,
        compiler_params=pltpu.CompilerParams(vmem_limit_bytes=4 * MIB),
        cost_estimate=pl.CostEstimate(flops=MIB, bytes_accessed=2 * MIB, transcendentals=0),
    )(*args)


def along_y(distance, cross=0):
    return [(i, ((i + (2 * distance if i % 2 == 0 else -2 * distance)) % 16) ^ cross) for i in range(16)]


CORES = [(i, i ^ 1) for i in range(16)]
HALVES = [(i, i ^ 1) for i in range(8)]


SHIFTS = (3, 1, 4, 2, 0)
OFFSETS = (0, 2, 1, -1)


def by_x(offset):
    pairs = []
    for ma in range(8):
        for ka in range(16):
            step = 2 if offset == 2 and ka % 2 == 0 else -offset
            pairs.append((ma * 16 + ka, ((ma + 2 * step) % 8) * 16 + ka))
    return pairs


def shards(left_matrix, right_panel):
    def from_row(b):
        return [b] + [lax.ppermute(b, ("ma", "ka"), by_x(offset)) for offset in OFFSETS[1:]]

    far_b = from_row(lax.ppermute(right_panel, "ma", HALVES))
    sums, a_high, a_low = early(left_matrix, from_row(right_panel))

    def rest(mine):
        return late(SHIFTS, mine, a_high, a_low, sums, far_b)

    three, four, one_own, one_other, two, zero = add(lax.ppermute(rest(False), "ka", CORES), rest(True))
    got_three = lax.ppermute(three, "ka", along_y(1))
    got_four = lax.ppermute(four, "ka", along_y(2))
    near_own = lax.ppermute(one_own, "ka", along_y(1))
    near_other = lax.ppermute(one_other, "ka", along_y(1, 1))

    own, other = halves(pass_on_kernel, two, got_three, got_four)
    far_own = lax.ppermute(own, "ka", along_y(2))
    far_other = lax.ppermute(other, "ka", along_y(2, 1))
    return zero + near_own + near_other + far_own + far_other


def solution(mesh):
    in_specs = (P("ma", "ka"), P(("ka", "ma"), "an"))
    out_specs = P(("ma", "ka"), "an")
    return jax.shard_map(shards, mesh=mesh, in_specs=in_specs, out_specs=out_specs, check_vma=False)
```

```python
import jax
import jax.numpy as jnp
from jax import lax
from jax.experimental import pallas as pl
from jax.experimental.pallas import tpu as pltpu
from jax.sharding import PartitionSpec as P

F32, BF16 = jnp.float32, jnp.bfloat16
VMEM = pl.BlockSpec(memory_space=pltpu.VMEM)
MIB = 1024 * 1024


def two_parts(value):
    high = value.astype(BF16)
    return high, (value - high.astype(F32)).astype(BF16)


def place():
    ka, ma = lax.axis_index("ka"), lax.axis_index("ma")
    return ka // 2, ka % 2, ma % 2, ma // 2


def dot(a, b):
    return jnp.dot(a, b, preferred_element_type=F32)


def place_parts(pieces, high, low):
    _, _, _, own_x = place()
    for offset, piece in zip(OFFSETS, pieces):
        rows = pl.ds(pl.multiple_of(((own_x + offset) % 4) * 128, 128), 128)
        high[rows, :], low[rows, :] = two_parts(piece[...])


def row_copies(a_hbm, a_ref, sems, mine):
    y, core, _, _ = place()
    side = core if mine else 1 - core
    copies, at = [], 0
    for index, shift in enumerate(SHIFTS):
        if shift in (0, 4):
            start, count = ((y + shift) % 8) * 256 + side * 128, 128
        else:
            start, count = ((y + jnp.where(side == 0, shift, 8 - shift)) % 8) * 256, 256
        rows = pl.ds(pl.multiple_of(start, 128), count)
        copies.append(pltpu.make_async_copy(a_hbm.at[rows], a_ref.at[pl.ds(at, count)], sems.at[index]))
        at += count
    return copies


def parts_of(a_ref, rows, z):
    return two_parts(jnp.concatenate([a_ref[rows, 256 * x + 128 * z : 256 * x + 128 * z + 128] for x in range(4)], axis=1))


def three_dots(high, low, b_high, b_low):
    return dot(high, b_low[...]) + dot(low, b_high[...]) + dot(high, b_high[...])


def for_each_tile(body, copies=None):
    _, _, half, _ = place()
    for z in range(2):

        @pl.when(half == z)
        def _(z=z):
            for step, needed in enumerate(((0,), (1,), (2,), (3, 4))):
                for index in needed if copies else ():
                    copies[index].wait()
                body(z, slice(256 * step, 256 * step + 256))


def early_kernel(a_hbm, b0, b1, b2, b3, sums, high_out, low_out, b_high, b_low, a_kept, a_ref, sems, kept_sems):
    copies, kept_copies = row_copies(a_hbm, a_ref, sems, False), row_copies(a_hbm, a_kept, kept_sems, True)
    for copy in copies + kept_copies:
        copy.start()
    place_parts((b0, b1, b2, b3), b_high, b_low)

    def body(z, rows):
        sums[rows, :] = three_dots(*parts_of(a_ref, rows, z), b_high, b_low)
        high_out[rows, :], low_out[rows, :] = parts_of(a_ref, rows, 1 - z)

    for_each_tile(body, copies)
    for copy in kept_copies:
        copy.wait()


def late_kernel(sums, a_high, a_low, b0, b1, b2, b3, out, b_high, b_low):
    place_parts((b0, b1, b2, b3), b_high, b_low)
    for step in range(4):
        rows = slice(256 * step, 256 * step + 256)
        out[rows, :] = sums[rows, :] + three_dots(a_high[rows, :], a_low[rows, :], b_high, b_low)


def whole_kernel(a_ref, near_high, near_low, far_high, far_low, out):
    def body(z, rows):
        near = three_dots(*parts_of(a_ref, rows, z), near_high, near_low)
        out[rows, :] = near + three_dots(*parts_of(a_ref, rows, 1 - z), far_high, far_low)

    for_each_tile(body)


def product(kernel, outs, reads_a, limit, *args):
    return pl.pallas_call(
        kernel,
        in_specs=[pl.BlockSpec(memory_space=pl.ANY) if reads_a else VMEM] + [VMEM] * (len(args) - 1),
        out_specs=[VMEM] * len(outs),
        out_shape=[jax.ShapeDtypeStruct(shape, kind) for shape, kind in outs],
        scratch_shapes=[pltpu.VMEM((1024, 1024), F32)] + [pltpu.SemaphoreType.DMA((5,))] * 2 if reads_a else [],
        compiler_params=pltpu.CompilerParams(vmem_limit_bytes=limit * MIB),
        cost_estimate=pl.CostEstimate(flops=2 * 3 * 1024 * 512 * 512, bytes_accessed=8 * MIB, transcendentals=0),
    )(*args)


def add_kernel(first, second, three, four, one_own, one_other, two, zero):
    _, core, _, _ = place()
    own, other = (pl.multiple_of(256 + side * 128, 128) for side in (core, 1 - core))
    for start, out in ((0, three), (own, one_own), (other, one_other), (512, two), (768, four), (896, zero)):
        rows = pl.ds(start, out.shape[0])
        out[...] = first[rows, :] + second[rows, :]


def add(first, second):
    counts = (256, 128, 128, 128, 256, 128)
    return pl.pallas_call(
        add_kernel,
        in_specs=[VMEM] * 2,
        out_specs=[VMEM] * len(counts),
        out_shape=[jax.ShapeDtypeStruct((count, 512), F32) for count in counts],
        compiler_params=pltpu.CompilerParams(vmem_limit_bytes=8 * MIB),
        cost_estimate=pl.CostEstimate(flops=MIB, bytes_accessed=4 * MIB, transcendentals=0),
    )(first, second)


def pass_on_kernel(two, got_three, got_four, own, other):
    _, core, _, _ = place()
    for index, out in ((core, own), (1 - core, other)):
        rows = pl.ds(pl.multiple_of(index * 128, 128), 128)
        total = two[rows, :] + got_three[rows, :]
        out[...] = total + got_four[...] if out is own else total


def halves(kernel, *args):
    return pl.pallas_call(
        kernel,
        in_specs=[VMEM] * len(args),
        out_specs=[VMEM] * 2,
        out_shape=[jax.ShapeDtypeStruct((128, 512), F32)] * 2,
        compiler_params=pltpu.CompilerParams(vmem_limit_bytes=4 * MIB),
        cost_estimate=pl.CostEstimate(flops=MIB, bytes_accessed=2 * MIB, transcendentals=0),
    )(*args)


def along_y(distance, cross=0):
    return [(i, ((i + (2 * distance if i % 2 == 0 else -2 * distance)) % 16) ^ cross) for i in range(16)]


CORES = [(i, i ^ 1) for i in range(16)]
HALVES = [(i, i ^ 1) for i in range(8)]


SHIFTS = (3, 1, 2, 4, 0)
OFFSETS = (0, 2, 1, -1)


def by_x(offset):
    pairs = []
    for ma in range(8):
        for ka in range(16):
            step = 2 if offset == 2 and ka % 2 == 0 else -offset
            pairs.append((ma * 16 + ka, ((ma + 2 * step) % 8) * 16 + ka))
    return pairs


def shards(left_matrix, right_panel):
    def other_half(b):
        return lax.ppermute(b, "ma", HALVES)

    def from_row(b, offsets):
        return [lax.ppermute(b, ("ma", "ka"), by_x(offset)) for offset in offsets]

    near_b = [right_panel] + from_row(right_panel, OFFSETS[1:])
    swapped = other_half(right_panel)
    far_b = [swapped, other_half(near_b[1])] + from_row(swapped, OFFSETS[2:])
    sums, parts, b_parts = ((1024, 512), F32), [((1024, 512), BF16)] * 2, [((512, 512), BF16)] * 2
    outs = [sums] + parts + b_parts + [((1024, 1024), F32)]
    first, a_high, a_low, near_high, near_low, a_kept = product(early_kernel, outs, True, 40, left_matrix, *near_b)
    given, far_high, far_low = product(late_kernel, [sums] + b_parts, False, 14, first, a_high, a_low, *far_b)
    kept = product(whole_kernel, [sums], False, 14, a_kept, near_high, near_low, far_high, far_low)[0]

    three, four, one_own, one_other, two, zero = add(lax.ppermute(given, "ka", CORES), kept)
    got_three = lax.ppermute(three, "ka", along_y(1))
    got_four = lax.ppermute(four, "ka", along_y(2))
    near_own = lax.ppermute(one_own, "ka", along_y(1))
    near_other = lax.ppermute(one_other, "ka", along_y(1, 1))

    own, other = halves(pass_on_kernel, two, got_three, got_four)
    far_own = lax.ppermute(own, "ka", along_y(2))
    far_other = lax.ppermute(other, "ka", along_y(2, 1))
    return zero + near_own + near_other + far_own + far_other


def solution(mesh):
    in_specs = (P("ma", "ka"), P(("ka", "ma"), "an"))
    out_specs = P(("ma", "ka"), "an")
    return jax.shard_map(shards, mesh=mesh, in_specs=in_specs, out_specs=out_specs, check_vma=False)
```

```python
import jax
import jax.numpy as jnp
from jax import lax
from jax.experimental import pallas as pl
from jax.experimental.pallas import tpu as pltpu
from jax.sharding import PartitionSpec as P

F32, BF16 = jnp.float32, jnp.bfloat16
VMEM = pl.BlockSpec(memory_space=pltpu.VMEM)
MIB = 1024 * 1024


def two_parts(value):
    high = value.astype(BF16)
    return high, (value - high.astype(F32)).astype(BF16)


def place():
    ka, ma = lax.axis_index("ka"), lax.axis_index("ma")
    return ka // 2, ka % 2, ma % 2, ma // 2


def dot(a, b):
    return jnp.dot(a, b, preferred_element_type=F32)


def place_parts(pieces, high, low):
    _, core, _, own_x = place()
    for offset, piece in zip(OFFSETS, pieces):
        x = (own_x + jnp.where(core == 0, offset, 4 - offset)) % 4
        rows = pl.ds(pl.multiple_of(x * 128, 128), 128)
        high[rows, :], low[rows, :] = two_parts(piece[...])


def row_copies(a_hbm, a_ref, sems, mine):
    y, core, _, _ = place()
    side = core if mine else 1 - core
    copies, at = [], 0
    for index, shift in enumerate(SHIFTS):
        if shift in (0, 4):
            start, count = ((y + shift) % 8) * 256 + side * 128, 128
        else:
            start, count = ((y + jnp.where(side == 0, shift, 8 - shift)) % 8) * 256, 256
        rows = pl.ds(pl.multiple_of(start, 128), count)
        copies.append(pltpu.make_async_copy(a_hbm.at[rows], a_ref.at[pl.ds(at, count)], sems.at[index]))
        at += count
    return copies


def parts_of(a_ref, rows, z):
    return two_parts(jnp.concatenate([a_ref[rows, 256 * x + 128 * z : 256 * x + 128 * z + 128] for x in range(4)], axis=1))


def three_dots(high, low, b_high, b_low):
    return dot(high, b_low[...]) + dot(low, b_high[...]) + dot(high, b_high[...])


def for_each_tile(body, copies=None):
    _, _, half, _ = place()
    for z in range(2):

        @pl.when(half == z)
        def _(z=z):
            for step, needed in enumerate(((0,), (1,), (2,), (3, 4))):
                for index in needed if copies else ():
                    copies[index].wait()
                body(z, slice(256 * step, 256 * step + 256))


def early_kernel(a_hbm, b0, b1, b2, b3, sums, high_out, low_out, b_high, b_low, a_kept, a_ref, sems, kept_sems):
    copies, kept_copies = row_copies(a_hbm, a_ref, sems, False), row_copies(a_hbm, a_kept, kept_sems, True)
    for copy in copies + kept_copies:
        copy.start()
    place_parts((b0, b1, b2, b3), b_high, b_low)

    def body(z, rows):
        sums[rows, :] = three_dots(*parts_of(a_ref, rows, z), b_high, b_low)
        high_out[rows, :], low_out[rows, :] = parts_of(a_ref, rows, 1 - z)

    for_each_tile(body, copies)
    for copy in kept_copies:
        copy.wait()


def late_kernel(sums, a_high, a_low, b0, b1, b2, b3, out, b_high, b_low):
    place_parts((b0, b1, b2, b3), b_high, b_low)
    for step in range(4):
        rows = slice(256 * step, 256 * step + 256)
        out[rows, :] = sums[rows, :] + three_dots(a_high[rows, :], a_low[rows, :], b_high, b_low)


def whole_kernel(a_ref, near_high, near_low, far_high, far_low, out):
    def body(z, rows):
        near = three_dots(*parts_of(a_ref, rows, z), near_high, near_low)
        out[rows, :] = near + three_dots(*parts_of(a_ref, rows, 1 - z), far_high, far_low)

    for_each_tile(body)


def product(kernel, outs, reads_a, limit, *args):
    return pl.pallas_call(
        kernel,
        in_specs=[pl.BlockSpec(memory_space=pl.ANY) if reads_a else VMEM] + [VMEM] * (len(args) - 1),
        out_specs=[VMEM] * len(outs),
        out_shape=[jax.ShapeDtypeStruct(shape, kind) for shape, kind in outs],
        scratch_shapes=[pltpu.VMEM((1024, 1024), F32)] + [pltpu.SemaphoreType.DMA((5,))] * 2 if reads_a else [],
        compiler_params=pltpu.CompilerParams(vmem_limit_bytes=limit * MIB),
        cost_estimate=pl.CostEstimate(flops=2 * 3 * 1024 * 512 * 512, bytes_accessed=8 * MIB, transcendentals=0),
    )(*args)


def add_kernel(first, second, three, four, one_own, one_other, two, zero):
    _, core, _, _ = place()
    own, other = (pl.multiple_of(256 + side * 128, 128) for side in (core, 1 - core))
    for start, out in ((0, three), (own, one_own), (other, one_other), (512, two), (768, four), (896, zero)):
        rows = pl.ds(start, out.shape[0])
        out[...] = first[rows, :] + second[rows, :]


def add(first, second):
    counts = (256, 128, 128, 128, 256, 128)
    return pl.pallas_call(
        add_kernel,
        in_specs=[VMEM] * 2,
        out_specs=[VMEM] * len(counts),
        out_shape=[jax.ShapeDtypeStruct((count, 512), F32) for count in counts],
        compiler_params=pltpu.CompilerParams(vmem_limit_bytes=8 * MIB),
        cost_estimate=pl.CostEstimate(flops=MIB, bytes_accessed=4 * MIB, transcendentals=0),
    )(first, second)


def pass_on_kernel(two, got_three, got_four, own, other):
    _, core, _, _ = place()
    for index, out in ((core, own), (1 - core, other)):
        rows = pl.ds(pl.multiple_of(index * 128, 128), 128)
        total = two[rows, :] + got_three[rows, :]
        out[...] = total + got_four[...] if out is own else total


def halves(kernel, *args):
    return pl.pallas_call(
        kernel,
        in_specs=[VMEM] * len(args),
        out_specs=[VMEM] * 2,
        out_shape=[jax.ShapeDtypeStruct((128, 512), F32)] * 2,
        compiler_params=pltpu.CompilerParams(vmem_limit_bytes=4 * MIB),
        cost_estimate=pl.CostEstimate(flops=MIB, bytes_accessed=2 * MIB, transcendentals=0),
    )(*args)


def along_y(distance, cross=0):
    return [(i, ((i + (2 * distance if i % 2 == 0 else -2 * distance)) % 16) ^ cross) for i in range(16)]


CORES = [(i, i ^ 1) for i in range(16)]
HALVES = [(i, i ^ 1) for i in range(8)]


SHIFTS = (3, 1, 2, 4, 0)
OFFSETS = (0, 2, 1, -1)


def by_x(offset):
    pairs = []
    for ma in range(8):
        for ka in range(16):
            step = -offset if ka % 2 == 0 else offset
            pairs.append((ma * 16 + ka, ((ma + 2 * step) % 8) * 16 + ka))
    return pairs


def shards(left_matrix, right_panel):
    def other_half(b):
        return lax.ppermute(b, "ma", HALVES)

    def from_row(b, offsets):
        return [lax.ppermute(b, ("ma", "ka"), by_x(offset)) for offset in offsets]

    near_b = [right_panel] + from_row(right_panel, OFFSETS[1:])
    swapped = other_half(right_panel)
    far_b = [swapped, other_half(near_b[1])] + from_row(swapped, OFFSETS[2:])
    sums, parts, b_parts = ((1024, 512), F32), [((1024, 512), BF16)] * 2, [((512, 512), BF16)] * 2
    outs = [sums] + parts + b_parts + [((1024, 1024), F32)]
    first, a_high, a_low, near_high, near_low, a_kept = product(early_kernel, outs, True, 40, left_matrix, *near_b)
    given, far_high, far_low = product(late_kernel, [sums] + b_parts, False, 14, first, a_high, a_low, *far_b)
    kept = product(whole_kernel, [sums], False, 14, a_kept, near_high, near_low, far_high, far_low)[0]

    three, four, one_own, one_other, two, zero = add(lax.ppermute(given, "ka", CORES), kept)
    got_three = lax.ppermute(three, "ka", along_y(1))
    got_four = lax.ppermute(four, "ka", along_y(2))
    near_own = lax.ppermute(one_own, "ka", along_y(1))
    near_other = lax.ppermute(one_other, "ka", along_y(1, 1))

    own, other = halves(pass_on_kernel, two, got_three, got_four)
    far_own = lax.ppermute(own, "ka", along_y(2))
    far_other = lax.ppermute(other, "ka", along_y(2, 1))
    return zero + near_own + near_other + far_own + far_other


def solution(mesh):
    in_specs = (P("ma", "ka"), P(("ka", "ma"), "an"))
    out_specs = P(("ma", "ka"), "an")
    return jax.shard_map(shards, mesh=mesh, in_specs=in_specs, out_specs=out_specs, check_vma=False)
```

```python
import jax
import jax.numpy as jnp
from jax import lax
from jax.experimental import pallas as pl
from jax.experimental.pallas import tpu as pltpu
from jax.sharding import PartitionSpec as P

F32, BF16 = jnp.float32, jnp.bfloat16
VMEM = pl.BlockSpec(memory_space=pltpu.VMEM)
MIB = 1024 * 1024


def two_parts(value):
    high = value.astype(BF16)
    return high, (value - high.astype(F32)).astype(BF16)


def place():
    ka, ma = lax.axis_index("ka"), lax.axis_index("ma")
    return ka // 2, ka % 2, ma % 2, ma // 2


def dot(a, b):
    return jnp.dot(a, b, preferred_element_type=F32)


def place_parts(pieces, high, low):
    _, core, _, own_x = place()
    for offset, piece in zip(OFFSETS, pieces):
        x = (own_x + jnp.where(core == 0, offset, 4 - offset)) % 4
        rows = pl.ds(pl.multiple_of(x * 128, 128), 128)
        high[rows, :], low[rows, :] = two_parts(piece[...])


def row_copies(a_hbm, a_ref, sems, mine):
    y, core, _, _ = place()
    side = core if mine else 1 - core
    copies, at = [], 0
    for index, shift in enumerate(SHIFTS):
        if shift in (0, 4):
            start, count = ((y + shift) % 8) * 256 + side * 128, 128
        else:
            start, count = ((y + jnp.where(side == 0, shift, 8 - shift)) % 8) * 256, 256
        rows = pl.ds(pl.multiple_of(start, 128), count)
        copies.append(pltpu.make_async_copy(a_hbm.at[rows], a_ref.at[pl.ds(at, count)], sems.at[index]))
        at += count
    return copies


def parts_of(a_ref, rows, z):
    return two_parts(jnp.concatenate([a_ref[rows, 256 * x + 128 * z : 256 * x + 128 * z + 128] for x in range(4)], axis=1))


def three_dots(high, low, b_high, b_low):
    return dot(high, b_low[...]) + dot(low, b_high[...]) + dot(high, b_high[...])


def for_each_tile(body, copies=None):
    _, _, half, _ = place()
    for z in range(2):

        @pl.when(half == z)
        def _(z=z):
            for step, needed in enumerate(((0,), (1,), (2,), (3, 4))):
                for index in needed if copies else ():
                    copies[index].wait()
                body(z, slice(256 * step, 256 * step + 256))


def early_kernel(a_hbm, b0, b1, b2, b3, sums, high_out, low_out, b_high, b_low, a_kept, a_ref, sems, kept_sems):
    copies, kept_copies = row_copies(a_hbm, a_ref, sems, False), row_copies(a_hbm, a_kept, kept_sems, True)
    for copy in copies + kept_copies:
        copy.start()
    place_parts((b0, b1, b2, b3), b_high, b_low)

    def body(z, rows):
        sums[rows, :] = three_dots(*parts_of(a_ref, rows, z), b_high, b_low)
        high_out[rows, :], low_out[rows, :] = parts_of(a_ref, rows, 1 - z)

    for_each_tile(body, copies)
    for copy in kept_copies:
        copy.wait()


def store(rows, value, out, zero_out):
    if rows.stop <= 896:
        out[rows, :] = value
    else:
        out[rows.start : 896, :] = value[:128]
        zero_out[...] = value[128:]


def late_kernel(sums, a_high, a_low, b0, b1, b2, b3, out, zero_out, b_high, b_low):
    place_parts((b0, b1, b2, b3), b_high, b_low)
    for step in range(4):
        rows = slice(256 * step, 256 * step + 256)
        value = sums[rows, :] + three_dots(a_high[rows, :], a_low[rows, :], b_high, b_low)
        store(rows, value, out, zero_out)


def whole_kernel(a_ref, near_high, near_low, far_high, far_low, out, zero_out):
    def body(z, rows):
        near = three_dots(*parts_of(a_ref, rows, z), near_high, near_low)
        store(rows, near + three_dots(*parts_of(a_ref, rows, 1 - z), far_high, far_low), out, zero_out)

    for_each_tile(body)


def product(kernel, outs, reads_a, limit, *args):
    return pl.pallas_call(
        kernel,
        in_specs=[pl.BlockSpec(memory_space=pl.ANY) if reads_a else VMEM] + [VMEM] * (len(args) - 1),
        out_specs=[VMEM] * len(outs),
        out_shape=[jax.ShapeDtypeStruct(shape, kind) for shape, kind in outs],
        scratch_shapes=[pltpu.VMEM((1024, 1024), F32)] + [pltpu.SemaphoreType.DMA((5,))] * 2 if reads_a else [],
        compiler_params=pltpu.CompilerParams(vmem_limit_bytes=limit * MIB),
        cost_estimate=pl.CostEstimate(flops=2 * 3 * 1024 * 512 * 512, bytes_accessed=8 * MIB, transcendentals=0),
    )(*args)


def add_kernel(first, second, three, four, one_own, one_other, two):
    _, core, _, _ = place()
    own, other = (pl.multiple_of(256 + side * 128, 128) for side in (core, 1 - core))
    for start, out in ((0, three), (own, one_own), (other, one_other), (512, two), (768, four)):
        rows = pl.ds(start, out.shape[0])
        out[...] = first[rows, :] + second[rows, :]


def add(first, second):
    counts = (256, 128, 128, 128, 256)
    return pl.pallas_call(
        add_kernel,
        in_specs=[VMEM] * 2,
        out_specs=[VMEM] * len(counts),
        out_shape=[jax.ShapeDtypeStruct((count, 512), F32) for count in counts],
        compiler_params=pltpu.CompilerParams(vmem_limit_bytes=8 * MIB),
        cost_estimate=pl.CostEstimate(flops=MIB, bytes_accessed=4 * MIB, transcendentals=0),
    )(first, second)


def pass_on_kernel(two, got_three, got_four, own, other):
    _, core, _, _ = place()
    for index, out in ((core, own), (1 - core, other)):
        rows = pl.ds(pl.multiple_of(index * 128, 128), 128)
        total = two[rows, :] + got_three[rows, :]
        out[...] = total + got_four[...] if out is own else total


def halves(kernel, *args):
    return pl.pallas_call(
        kernel,
        in_specs=[VMEM] * len(args),
        out_specs=[VMEM] * 2,
        out_shape=[jax.ShapeDtypeStruct((128, 512), F32)] * 2,
        compiler_params=pltpu.CompilerParams(vmem_limit_bytes=4 * MIB),
        cost_estimate=pl.CostEstimate(flops=MIB, bytes_accessed=2 * MIB, transcendentals=0),
    )(*args)


def along_y(distance, cross=0):
    return [(i, ((i + (2 * distance if i % 2 == 0 else -2 * distance)) % 16) ^ cross) for i in range(16)]


CORES = [(i, i ^ 1) for i in range(16)]
HALVES = [(i, i ^ 1) for i in range(8)]


SHIFTS = (3, 1, 2, 4, 0)
OFFSETS = (0, 2, 1, -1)


def by_x(offset):
    pairs = []
    for ma in range(8):
        for ka in range(16):
            step = -offset if ka % 2 == 0 else offset
            pairs.append((ma * 16 + ka, ((ma + 2 * step) % 8) * 16 + ka))
    return pairs


def shards(left_matrix, right_panel):
    def other_half(b):
        return lax.ppermute(b, "ma", HALVES)

    def from_row(b, offsets):
        return [lax.ppermute(b, ("ma", "ka"), by_x(offset)) for offset in offsets]

    near_b = [right_panel] + from_row(right_panel, OFFSETS[1:])
    swapped = other_half(right_panel)
    far_b = [swapped, other_half(near_b[1])] + from_row(swapped, OFFSETS[2:])
    sums, parts, b_parts = ((1024, 512), F32), [((1024, 512), BF16)] * 2, [((512, 512), BF16)] * 2
    outs = [sums] + parts + b_parts + [((1024, 1024), F32)]
    first, a_high, a_low, near_high, near_low, a_kept = product(early_kernel, outs, True, 40, left_matrix, *near_b)
    swapped_sums = [((896, 512), F32), ((128, 512), F32)]
    given, zero_given, far_high, far_low = product(late_kernel, swapped_sums + b_parts, False, 14, first, a_high, a_low, *far_b)
    kept, zero = product(whole_kernel, swapped_sums, False, 14, a_kept, near_high, near_low, far_high, far_low)

    three, four, one_own, one_other, two = add(lax.ppermute(given, "ka", CORES), kept)
    got_three = lax.ppermute(three, "ka", along_y(1))
    got_four = lax.ppermute(four, "ka", along_y(2))
    near_own = lax.ppermute(one_own, "ka", along_y(1))
    near_other = lax.ppermute(one_other, "ka", along_y(1, 1))

    own, other = halves(pass_on_kernel, two, got_three, got_four)
    far_own = lax.ppermute(own, "ka", along_y(2))
    far_other = lax.ppermute(other, "ka", along_y(2, 1))
    zero_got = lax.ppermute(zero_given, "ka", CORES)
    return zero + zero_got + near_own + near_other + far_own + far_other


def solution(mesh):
    in_specs = (P("ma", "ka"), P(("ka", "ma"), "an"))
    out_specs = P(("ma", "ka"), "an")
    return jax.shard_map(shards, mesh=mesh, in_specs=in_specs, out_specs=out_specs, check_vma=False)
```

```python
import jax
import jax.numpy as jnp
from jax import lax
from jax.experimental import pallas as pl
from jax.experimental.pallas import tpu as pltpu
from jax.sharding import PartitionSpec as P

F32, BF16 = jnp.float32, jnp.bfloat16
VMEM = pl.BlockSpec(memory_space=pltpu.VMEM)
MIB = 1024 * 1024


def two_parts(value):
    high = value.astype(BF16)
    return high, (value - high.astype(F32)).astype(BF16)


def place():
    ka, ma = lax.axis_index("ka"), lax.axis_index("ma")
    return ka // 2, ka % 2, ma % 2, ma // 2


def dot(a, b):
    return jnp.dot(a, b, preferred_element_type=F32)


def place_parts(pieces, high, low):
    _, core, _, own_x = place()
    for offset, piece in zip(OFFSETS, pieces):
        x = (own_x + jnp.where(core == 0, offset, 4 - offset)) % 4
        rows = pl.ds(pl.multiple_of(x * 128, 128), 128)
        high[rows, :], low[rows, :] = two_parts(piece[...])


def row_copies(a_hbm, a_ref, sems, mine):
    y, core, _, _ = place()
    side = core if mine else 1 - core
    copies, at = [], 0
    for index, shift in enumerate(SHIFTS):
        if shift in (0, 4):
            start, count = ((y + shift) % 8) * 256 + side * 128, 128
        else:
            start, count = ((y + jnp.where(side == 0, shift, 8 - shift)) % 8) * 256, 256
        rows = pl.ds(pl.multiple_of(start, 128), count)
        copies.append(pltpu.make_async_copy(a_hbm.at[rows], a_ref.at[pl.ds(at, count)], sems.at[index]))
        at += count
    return copies


def parts_of(a_ref, rows, z):
    return two_parts(jnp.concatenate([a_ref[rows, 256 * x + 128 * z : 256 * x + 128 * z + 128] for x in range(4)], axis=1))


def three_dots(high, low, b_high, b_low):
    return dot(high, b_low[...]) + dot(low, b_high[...]) + dot(high, b_high[...])


def for_each_tile(body, copies=None):
    _, _, half, _ = place()
    for z in range(2):

        @pl.when(half == z)
        def _(z=z):
            for step, needed in enumerate(((0,), (1,), (2,), (3, 4))):
                for index in needed if copies else ():
                    copies[index].wait()
                body(z, slice(256 * step, 256 * step + 256))


def early_kernel(a_hbm, b0, b1, b2, b3, sums, high_out, low_out, b_high, b_low, a_kept, a_ref, sems, kept_sems):
    copies, kept_copies = row_copies(a_hbm, a_ref, sems, False), row_copies(a_hbm, a_kept, kept_sems, True)
    for copy in copies + kept_copies:
        copy.start()
    place_parts((b0, b1, b2, b3), b_high, b_low)

    def body(z, rows):
        sums[rows, :] = three_dots(*parts_of(a_ref, rows, z), b_high, b_low)
        high_out[rows, :], low_out[rows, :] = parts_of(a_ref, rows, 1 - z)

    for_each_tile(body, copies)
    for copy in kept_copies:
        copy.wait()


def late_kernel(sums, a_high, a_low, b0, b1, b2, b3, out, b_high, b_low):
    place_parts((b0, b1, b2, b3), b_high, b_low)
    for step in range(4):
        rows = slice(256 * step, 256 * step + 256)
        out[rows, :] = sums[rows, :] + three_dots(a_high[rows, :], a_low[rows, :], b_high, b_low)


def whole_kernel(a_ref, near_high, near_low, far_high, far_low, out):
    def body(z, rows):
        near = three_dots(*parts_of(a_ref, rows, z), near_high, near_low)
        out[rows, :] = near + three_dots(*parts_of(a_ref, rows, 1 - z), far_high, far_low)

    for_each_tile(body)


def product(kernel, outs, reads_a, limit, *args):
    return pl.pallas_call(
        kernel,
        in_specs=[pl.BlockSpec(memory_space=pl.ANY) if reads_a else VMEM] + [VMEM] * (len(args) - 1),
        out_specs=[VMEM] * len(outs),
        out_shape=[jax.ShapeDtypeStruct(shape, kind) for shape, kind in outs],
        scratch_shapes=[pltpu.VMEM((1024, 1024), F32)] + [pltpu.SemaphoreType.DMA((5,))] * 2 if reads_a else [],
        compiler_params=pltpu.CompilerParams(vmem_limit_bytes=limit * MIB),
        cost_estimate=pl.CostEstimate(flops=2 * 3 * 1024 * 512 * 512, bytes_accessed=8 * MIB, transcendentals=0),
    )(*args)


def add_kernel(first, second, *outs):
    _, core, _, _ = place()
    starts = [pl.multiple_of(256 * block + side * 128, 128) for block in range(3) for side in (core, 1 - core)]
    for start, out in zip(starts + [768, 896], outs):
        rows = pl.ds(start, 128)
        out[...] = first[rows, :] + second[rows, :]


def add(first, second):
    counts = (128,) * 8
    return pl.pallas_call(
        add_kernel,
        in_specs=[VMEM] * 2,
        out_specs=[VMEM] * len(counts),
        out_shape=[jax.ShapeDtypeStruct((count, 512), F32) for count in counts],
        compiler_params=pltpu.CompilerParams(vmem_limit_bytes=8 * MIB),
        cost_estimate=pl.CostEstimate(flops=MIB, bytes_accessed=4 * MIB, transcendentals=0),
    )(first, second)


def along_y(distance, cross=0):
    return [(i, ((i + (2 * distance if i % 2 == 0 else -2 * distance)) % 16) ^ cross) for i in range(16)]


CORES = [(i, i ^ 1) for i in range(16)]
HALVES = [(i, i ^ 1) for i in range(8)]


SHIFTS = (3, 1, 2, 4, 0)
OFFSETS = (0, 2, 1, -1)


def by_x(offset):
    pairs = []
    for ma in range(8):
        for ka in range(16):
            step = -offset if ka % 2 == 0 else offset
            pairs.append((ma * 16 + ka, ((ma + 2 * step) % 8) * 16 + ka))
    return pairs


def shards(left_matrix, right_panel):
    def other_half(b):
        return lax.ppermute(b, "ma", HALVES)

    def from_row(b, offsets):
        return [lax.ppermute(b, ("ma", "ka"), by_x(offset)) for offset in offsets]

    near_b = [right_panel] + from_row(right_panel, OFFSETS[1:])
    swapped = other_half(right_panel)
    far_b = [swapped, other_half(near_b[1])] + from_row(swapped, OFFSETS[2:])
    sums, parts, b_parts = ((1024, 512), F32), [((1024, 512), BF16)] * 2, [((512, 512), BF16)] * 2
    outs = [sums] + parts + b_parts + [((1024, 1024), F32)]
    first, a_high, a_low, near_high, near_low, a_kept = product(early_kernel, outs, True, 40, left_matrix, *near_b)
    given, far_high, far_low = product(late_kernel, [sums] + b_parts, False, 14, first, a_high, a_low, *far_b)
    kept = product(whole_kernel, [sums], False, 14, a_kept, near_high, near_low, far_high, far_low)[0]

    three_own, three_other, one_own, one_other, two_own, two_other, four, zero = add(
        lax.ppermute(given, "ka", CORES), kept
    )
    got_three_other = lax.ppermute(three_other, "ka", along_y(1))
    got_four = lax.ppermute(four, "ka", along_y(2))
    got_three_own = lax.ppermute(three_own, "ka", along_y(1))
    got_two_other = lax.ppermute(two_other + got_three_other, "ka", along_y(1))
    near_own = lax.ppermute(one_own, "ka", along_y(1))
    far_own = lax.ppermute(two_own + got_three_own + got_four, "ka", along_y(2))
    far_other = lax.ppermute(one_other + got_two_other, "ka", along_y(1, 1))
    return zero + near_own + far_own + far_other


def solution(mesh):
    in_specs = (P("ma", "ka"), P(("ka", "ma"), "an"))
    out_specs = P(("ma", "ka"), "an")
    return jax.shard_map(shards, mesh=mesh, in_specs=in_specs, out_specs=out_specs, check_vma=False)
```

```python
import jax
import jax.numpy as jnp
from jax import lax
from jax.experimental import pallas as pl
from jax.experimental.pallas import tpu as pltpu
from jax.sharding import PartitionSpec as P

F32, BF16 = jnp.float32, jnp.bfloat16
VMEM = pl.BlockSpec(memory_space=pltpu.VMEM)
MIB = 1024 * 1024


def two_parts(value):
    high = value.astype(BF16)
    return high, (value - high.astype(F32)).astype(BF16)


def place():
    ka, ma = lax.axis_index("ka"), lax.axis_index("ma")
    return ka // 2, ka % 2, ma % 2, ma // 2


def dot(a, b):
    return jnp.dot(a, b, preferred_element_type=F32)


def place_parts(pieces, high, low):
    _, core, _, own_x = place()
    for offset, piece in zip(OFFSETS, pieces):
        x = (own_x + jnp.where(core == 0, offset, 4 - offset)) % 4
        rows = pl.ds(pl.multiple_of(x * 128, 128), 128)
        high[rows, :], low[rows, :] = two_parts(piece[...])


def row_copies(a_hbm, a_ref, sems, mine):
    y, core, _, _ = place()
    side = core if mine else 1 - core
    copies, at = [], 0
    for index, shift in enumerate(SHIFTS):
        if shift in (0, 4):
            start, count = ((y + shift) % 8) * 256 + side * 128, 128
        else:
            start, count = ((y + jnp.where(side == 0, shift, 8 - shift)) % 8) * 256, 256
        rows = pl.ds(pl.multiple_of(start, 128), count)
        copies.append(pltpu.make_async_copy(a_hbm.at[rows], a_ref.at[pl.ds(at, count)], sems.at[index]))
        at += count
    return copies


def parts_of(a_ref, rows, z):
    return two_parts(jnp.concatenate([a_ref[rows, 256 * x + 128 * z : 256 * x + 128 * z + 128] for x in range(4)], axis=1))


def three_dots(high, low, b_high, b_low):
    return dot(high, b_low[...]) + dot(low, b_high[...]) + dot(high, b_high[...])


def for_each_tile(body, copies=None):
    _, _, half, _ = place()
    for z in range(2):

        @pl.when(half == z)
        def _(z=z):
            for step, needed in enumerate(((0,), (1,), (2,), (3, 4))):
                for index in needed if copies else ():
                    copies[index].wait()
                body(z, slice(256 * step, 256 * step + 256))


def early_kernel(a_hbm, b0, b1, b2, b3, sums, high_out, low_out, b_high, b_low, a_kept, a_ref, sems, kept_sems):
    copies, kept_copies = row_copies(a_hbm, a_ref, sems, False), row_copies(a_hbm, a_kept, kept_sems, True)
    for copy in copies + kept_copies:
        copy.start()
    place_parts((b0, b1, b2, b3), b_high, b_low)

    def body(z, rows):
        sums[rows, :] = three_dots(*parts_of(a_ref, rows, z), b_high, b_low)
        high_out[rows, :], low_out[rows, :] = parts_of(a_ref, rows, 1 - z)

    for_each_tile(body, copies)
    for copy in kept_copies:
        copy.wait()


def store(rows, value, out, zero_out):
    if rows.stop <= 896:
        out[rows, :] = value
    else:
        out[rows.start : 896, :] = value[:128]
        zero_out[...] = value[128:]


def late_kernel(sums, a_high, a_low, b0, b1, b2, b3, out, zero_out, b_high, b_low):
    place_parts((b0, b1, b2, b3), b_high, b_low)
    for step in range(4):
        rows = slice(256 * step, 256 * step + 256)
        value = sums[rows, :] + three_dots(a_high[rows, :], a_low[rows, :], b_high, b_low)
        store(rows, value, out, zero_out)


def whole_kernel(a_ref, near_high, near_low, far_high, far_low, out, zero_out):
    def body(z, rows):
        near = three_dots(*parts_of(a_ref, rows, z), near_high, near_low)
        store(rows, near + three_dots(*parts_of(a_ref, rows, 1 - z), far_high, far_low), out, zero_out)

    for_each_tile(body)


def product(kernel, outs, reads_a, limit, *args):
    return pl.pallas_call(
        kernel,
        in_specs=[pl.BlockSpec(memory_space=pl.ANY) if reads_a else VMEM] + [VMEM] * (len(args) - 1),
        out_specs=[VMEM] * len(outs),
        out_shape=[jax.ShapeDtypeStruct(shape, kind) for shape, kind in outs],
        scratch_shapes=[pltpu.VMEM((1024, 1024), F32)] + [pltpu.SemaphoreType.DMA((5,))] * 2 if reads_a else [],
        compiler_params=pltpu.CompilerParams(vmem_limit_bytes=limit * MIB),
        cost_estimate=pl.CostEstimate(flops=2 * 3 * 1024 * 512 * 512, bytes_accessed=8 * MIB, transcendentals=0),
    )(*args)


def add_kernel(first, second, *outs):
    _, core, _, _ = place()
    starts = [pl.multiple_of(256 * block + side * 128, 128) for block in range(3) for side in (core, 1 - core)]
    for start, out in zip(starts + [768], outs):
        rows = pl.ds(start, 128)
        out[...] = first[rows, :] + second[rows, :]


def add(first, second):
    counts = (128,) * 7
    return pl.pallas_call(
        add_kernel,
        in_specs=[VMEM] * 2,
        out_specs=[VMEM] * len(counts),
        out_shape=[jax.ShapeDtypeStruct((count, 512), F32) for count in counts],
        compiler_params=pltpu.CompilerParams(vmem_limit_bytes=8 * MIB),
        cost_estimate=pl.CostEstimate(flops=MIB, bytes_accessed=4 * MIB, transcendentals=0),
    )(first, second)


def along_y(distance, cross=0):
    return [(i, ((i + (2 * distance if i % 2 == 0 else -2 * distance)) % 16) ^ cross) for i in range(16)]


CORES = [(i, i ^ 1) for i in range(16)]
HALVES = [(i, i ^ 1) for i in range(8)]


SHIFTS = (3, 1, 2, 4, 0)
OFFSETS = (0, 2, 1, -1)


def by_x(offset):
    pairs = []
    for ma in range(8):
        for ka in range(16):
            step = -offset if ka % 2 == 0 else offset
            pairs.append((ma * 16 + ka, ((ma + 2 * step) % 8) * 16 + ka))
    return pairs


def shards(left_matrix, right_panel):
    def other_half(b):
        return lax.ppermute(b, "ma", HALVES)

    def from_row(b, offsets):
        return [lax.ppermute(b, ("ma", "ka"), by_x(offset)) for offset in offsets]

    near_b = [right_panel] + from_row(right_panel, OFFSETS[1:])
    swapped = other_half(right_panel)
    far_b = [swapped, other_half(near_b[1])] + from_row(swapped, OFFSETS[2:])
    sums, parts, b_parts = ((1024, 512), F32), [((1024, 512), BF16)] * 2, [((512, 512), BF16)] * 2
    outs = [sums] + parts + b_parts + [((1024, 1024), F32)]
    first, a_high, a_low, near_high, near_low, a_kept = product(early_kernel, outs, True, 40, left_matrix, *near_b)
    swapped_sums = [((896, 512), F32), ((128, 512), F32)]
    given, zero_given, far_high, far_low = product(late_kernel, swapped_sums + b_parts, False, 14, first, a_high, a_low, *far_b)
    kept, zero = product(whole_kernel, swapped_sums, False, 14, a_kept, near_high, near_low, far_high, far_low)

    three_own, three_other, one_own, one_other, two_own, two_other, four = add(
        lax.ppermute(given, "ka", CORES), kept
    )
    got_three_other = lax.ppermute(three_other, "ka", along_y(1))
    got_three_own = lax.ppermute(three_own, "ka", along_y(1))
    got_four = lax.ppermute(four, "ka", along_y(2))
    got_two_other = lax.ppermute(two_other + got_three_other, "ka", along_y(1))
    near_own = lax.ppermute(one_own, "ka", along_y(1))
    far_own = lax.ppermute(two_own + got_three_own + got_four, "ka", along_y(2))
    far_other = lax.ppermute(one_other + got_two_other, "ka", along_y(1, 1))
    zero_got = lax.ppermute(zero_given, "ka", CORES)
    return zero + zero_got + near_own + far_own + far_other


def solution(mesh):
    in_specs = (P("ma", "ka"), P(("ka", "ma"), "an"))
    out_specs = P(("ma", "ka"), "an")
    return jax.shard_map(shards, mesh=mesh, in_specs=in_specs, out_specs=out_specs, check_vma=False)
```
